32 devices in a mesh: row: 4 (over y, x), col: 8 (over z, core).
Axes of the slice: x: 2, y: 2, z: 4, core: 2. Of those that a mesh axis runs over, the one named last changes fastest.
Arguments:
- measurement_tiling_settings: bfloat16 [16384, 40], P(('row', 'col')), may hold values from -4.875 to 4.875
- dest: int32 [16384], P(('row', 'col')), may hold values from 0 to 16383, as said below
- column_tiling_settings: bfloat16 [8192, 40], P('col'), may hold values from -4.875 to 4.875
- entry_layer_weight: bfloat16 [40, 2048], replicated, may hold values from -1 to 1
- entry_layer_bias: float32 [2048], replicated, may hold values from -3 to 3
- middle_layer_weight: bfloat16 [2048, 2048], replicated, may hold values from -0.1875 to 0.1875
- middle_layer_bias: float32 [2048], replicated, may hold values from -3 to 3
- output_layer_weight: bfloat16 [2048, 256], replicated, may hold values from -0.1875 to 0.1875
- relevance_weight_vector: float32 [256], replicated, may hold values from 0.015625 to 0.03125
- probes: float32 [8192, 64], P('col'), may hold values from -2.6516504 to 2.6516504
Outputs:
- product: float32 [16384, 64], P(('row', 'col'))
The draws below stay inside these ranges and needn't reach their ends.
Inputs may be any that keep to these rules, and one draw needn't show every extreme that they name: dest is a permutation of 0 to 16383, and the measurements held by one device go in equal numbers to the row positions of every device, 16 to each.
All inputs are finite; a program needn't handle non-finite values.
Results may differ from the reference program's by a relative error of at most 0.0088.
Values may be sent and summed in bfloat16 or wider, within the bound.
A program may use at most 64 MiB of HBM per device.

```python
import math
import jax
import jax.numpy as jnp
from jax import lax

INPUT_DIMENSION = 40
HID = 2048
FEAT = 256
PROBES = 64
R_DEV = 512
KERNEL_ROW_COUNT = 16384
NC = 8192
N_ROW = 4
N_COL = 8


def draw_dest(key, part):
    devices_all = N_ROW * N_COL
    share = R_DEV // devices_all
    first_key, second_key = jax.random.split(jax.random.fold_in(key, 11))
    sigma = jax.vmap(lambda one: jax.random.permutation(one, R_DEV))(jax.random.split(first_key, devices_all))
    tau = jax.vmap(lambda one: jax.random.permutation(one, R_DEV))(jax.random.split(second_key, devices_all))
    target = sigma % devices_all
    sub_slot = sigma // devices_all
    source = jnp.arange(devices_all, dtype=jnp.int32)[:, None]
    slot = source * share + sub_slot
    final = target * R_DEV + tau[target, slot]
    return final.reshape(-1).astype(jnp.int32)


def tiling_values(key, own_key, count):
    values = jnp.clip(1.4 * jax.random.normal(own_key, (count, INPUT_DIMENSION), jnp.float32), -4.875, 4.875)
    return values.astype(jnp.bfloat16)


def draw_measurement_tiling_settings(key, part):
    return tiling_values(key, jax.random.fold_in(key, 21), KERNEL_ROW_COUNT)


def draw_column_tiling_settings(key, part):
    return tiling_values(key, jax.random.fold_in(key, 22), NC)


def levels(key, dims, shards, smallest, largest):
    def one(position, shards_of):
        draws = jax.random.uniform(jax.random.fold_in(jax.random.fold_in(key, 6), position), (shards_of,), jnp.float32, smallest / len(shards), largest / len(shards))
        return jnp.repeat(jnp.exp(draws), dims[position] // shards_of).reshape((-1,) + (1,) * (len(dims) - position - 1))

    gain = one(*shards[0])
    for cut in shards[1:]:
        gain = gain * one(*cut)
    return gain


def gaussian(key, shape, scale, reach, cuts=(), kind=jnp.bfloat16):
    level = levels(key, shape, cuts, -0.22, 0.18) if cuts else 1.0
    values = jax.random.normal(key, shape, jnp.float32) * scale * level
    return jnp.minimum(jnp.maximum(values, -reach), reach).astype(kind)


def setup_inputs(seed: int = 0) -> dict:
    key_of = jax.random.split(jax.random.key(seed), 11)
    return {
        "measurement_tiling_settings": draw_measurement_tiling_settings(jax.random.fold_in(key_of[10], 71), 0),
        "dest": draw_dest(jax.random.fold_in(key_of[10], 71), 0),
        "column_tiling_settings": draw_column_tiling_settings(jax.random.fold_in(key_of[10], 71), 0),
        "entry_layer_weight": gaussian(key_of[3], (INPUT_DIMENSION, HID), INPUT_DIMENSION ** -0.5, 1.0),
        "entry_layer_bias": gaussian(key_of[4], (HID,), 0.5, 3.0, (), jnp.float32),
        "middle_layer_weight": gaussian(key_of[5], (HID, HID), (HID // 2) ** -0.5, 0.1875),
        "middle_layer_bias": gaussian(key_of[6], (HID,), 0.5, 3.0, (), jnp.float32),
        "output_layer_weight": gaussian(key_of[7], (HID, FEAT), (HID // 2) ** -0.5, 0.1875),
        "relevance_weight_vector": jnp.clip(jnp.exp(jax.random.uniform(key_of[8], (FEAT,), jnp.float32, math.log(0.015625), math.log(0.03125))), 0.015625, 0.03125),
        "probes": gaussian(key_of[9], (NC, PROBES), (40.0 / NC ** 0.5), 2.6516504, ((0, 8),), jnp.float32),
    }


def feature_extractor(inputs, entry_layer_weight, entry_layer_bias, middle_layer_weight, middle_layer_bias, output_layer_weight):
    hidden = jnp.maximum(jnp.dot(inputs, entry_layer_weight, preferred_element_type=jnp.float32) + entry_layer_bias, 0.0).astype(jnp.bfloat16)
    hidden = jnp.maximum(jnp.dot(hidden, middle_layer_weight, preferred_element_type=jnp.float32) + middle_layer_bias, 0.0).astype(jnp.bfloat16)
    return jnp.dot(hidden, output_layer_weight, preferred_element_type=jnp.float32).astype(jnp.bfloat16)


def reference(measurement_tiling_settings, dest, column_tiling_settings, entry_layer_weight, entry_layer_bias, middle_layer_weight, middle_layer_bias, output_layer_weight, relevance_weight_vector, probes):
    measurement_feature_rows = feature_extractor(measurement_tiling_settings, entry_layer_weight, entry_layer_bias, middle_layer_weight, middle_layer_bias, output_layer_weight)
    col_feats = feature_extractor(column_tiling_settings, entry_layer_weight, entry_layer_bias, middle_layer_weight, middle_layer_bias, output_layer_weight)
    source_row_index = jnp.zeros((KERNEL_ROW_COUNT,), jnp.int32).at[dest].set(jnp.arange(KERNEL_ROW_COUNT, dtype=jnp.int32))
    row_feature_matrix = measurement_feature_rows[source_row_index]
    scaled = (row_feature_matrix.astype(jnp.float32) * relevance_weight_vector).astype(jnp.bfloat16)
    sq_row = jnp.sum(relevance_weight_vector * jnp.square(row_feature_matrix.astype(jnp.float32)), axis=1)
    sq_col = jnp.sum(relevance_weight_vector * jnp.square(col_feats.astype(jnp.float32)), axis=1)
    block_rows = min(512, KERNEL_ROW_COUNT)
    blocks = KERNEL_ROW_COUNT // block_rows

    def one_block(pieces):
        scaled_rows, sq_rows = pieces
        cross = lax.dot_general(scaled_rows, col_feats, (((1,), (1,)), ((), ())), preferred_element_type=jnp.float32)
        kern = jnp.exp(-0.5 * (sq_rows[:, None] + sq_col[None, :] - 2.0 * cross))
        return jnp.dot(kern, probes, precision=lax.Precision.HIGHEST, preferred_element_type=jnp.float32)

    result = lax.map(one_block, (scaled.reshape(blocks, block_rows, FEAT), sq_row.reshape(blocks, block_rows)))
    return result.reshape(KERNEL_ROW_COUNT, PROBES)
```

```python
import functools

import jax
import jax.numpy as jnp
from jax import lax
from jax.experimental import pallas as pl
from jax.experimental.pallas import tpu as pltpu
from jax.sharding import PartitionSpec as P

BF = jnp.bfloat16
F32 = jnp.float32
NN = (((1,), (0,)), ((), ()))
NT = (((1,), (1,)), ((), ()))
TN = (((0,), (0,)), ((), ()))
MESH = pl.DeviceIdType.MESH
CHUNKS = 4


def mm(a, b, dims=NN):
    return lax.dot_general(a, b, dims, preferred_element_type=F32)


def kernel(
    n_row, n_col, slot,
    x_ref, dest_ref, cx_ref, w1_ref, b1_ref, w2_hbm, b2_ref, w3_hbm, rel_ref, probes_ref,
    out_ref,
    w2, w3, h1, h2, sent, got, colg, rowf, scaled, half_row, acc, part, parts_in,
    w_sem, a_send, a_recv, c_send, c_recv, f_send, r_send, r_recv, p_send, p_recv,
):
    n_dev = n_row * n_col
    rows, width = x_ref.shape
    hid = w1_ref.shape[1]
    feat = w3.shape[1]
    npr = probes_ref.shape[1]
    cols = cx_ref.shape[0] // n_row
    step = hid // CHUNKS
    slots = n_dev * slot
    mr, mc = lax.axis_index("row"), lax.axis_index("col")
    me = mr * n_col + mc
    core, chip, n_chip = mc % 2, mc // 2, n_col // 2
    sibling = mc + 1 - 2 * core

    w_copies = [
        pltpu.make_async_copy(w2_hbm.at[:, pl.ds(n * step, step)], w2.at[n], w_sem.at[n])
        for n in range(CHUNKS)
    ]
    w_copies.append(pltpu.make_async_copy(w3_hbm, w3, w_sem.at[CHUNKS]))
    for one in w_copies:
        one.start()

    barrier = pltpu.get_barrier_semaphore()

    @pl.loop(1, n_dev)
    def _(off):
        to = (me + off) % n_dev
        pl.semaphore_signal(
            barrier, inc=1, device_id=(to // n_col, to % n_col), device_id_type=MESH
        )

    bits = rows.bit_length() - 1
    dest = dest_ref[...]
    target = lax.shift_right_logical(dest, jnp.full_like(dest, bits))
    place = lax.bitwise_and(dest, jnp.full_like(dest, rows - 1)) + 1
    one_hot = (lax.broadcasted_iota(jnp.int32, (n_dev, rows), 0) == target).astype(F32)
    before = (
        lax.broadcasted_iota(jnp.int32, (rows, rows), 0)
        < lax.broadcasted_iota(jnp.int32, (rows, rows), 1)
    ).astype(F32).astype(BF)
    count = mm(one_hot.astype(BF), before)
    within = jnp.sum(one_hot * count, axis=0, keepdims=True)
    key = target * slot + within.astype(jnp.int32)
    pick = (lax.broadcasted_iota(jnp.int32, (slots, rows), 0) == key).astype(F32).astype(BF)
    high = lax.shift_right_logical(place, jnp.full_like(place, 5)).astype(F32)
    low = lax.bitwise_and(place, jnp.full_like(place, 31)).astype(F32)
    line = lax.broadcasted_iota(jnp.int32, (128, rows), 0)
    marks = jnp.where(line == width, high, jnp.where(line == width + 1, low, 0.0)).astype(BF)
    sent[...] = mm(pick, marks, NT).astype(BF).reshape(n_dev, slot, 128)
    sent[:, :, :width] = mm(pick, x_ref[...]).astype(BF).reshape(n_dev, slot, width)
    got[me] = sent[me]

    pl.semaphore_wait(barrier, n_dev - 1)

    def a2a(to, sem_at):
        return pltpu.make_async_remote_copy(
            src_ref=sent.at[to], dst_ref=got.at[sem_at],
            send_sem=a_send.at[to], recv_sem=a_recv.at[sem_at],
            device_id=(to // n_col, to % n_col), device_id_type=MESH,
        )

    @pl.loop(1, n_dev)
    def _(off):
        a2a((me + off) % n_dev, me).start()

    def layers(x, m, first, between=None):
        for n in range(CHUNKS):
            at = pl.ds(n * step, step)
            h1[:m, at] = jnp.maximum(mm(x, w1_ref[:, at]) + b1_ref[:, at], 0.0).astype(BF)
        if first:
            for one in w_copies[:CHUNKS]:
                one.wait()

        @pl.loop(0, CHUNKS)
        def _(n):
            at = pl.ds(pl.multiple_of(n * step, step), step)
            h2[:m, at] = jnp.maximum(mm(h1[:m, :], w2[n]) + b2_ref[:, at], 0.0).astype(BF)

        if first:
            w_copies[CHUNKS].wait()
        if between is not None:
            between()
        return mm(h2[:m, :], w3[...]).astype(BF)

    mine = pl.ds(pl.multiple_of(mr * cols, cols), cols)
    rel = rel_ref[...]
    cf = layers(cx_ref[mine, :], cols, True)
    colg[mc, :cols, :] = cf
    eye = (
        lax.broadcasted_iota(jnp.int32, (cols, cols), 0)
        == lax.broadcasted_iota(jnp.int32, (cols, cols), 1)
    ).astype(F32).astype(BF)
    colg[mc, pl.ds(cols, npr), :] = mm(probes_ref[mine, :].astype(BF), eye, TN).astype(BF)
    cf32 = cf.astype(F32)
    half_col = lax.dot_general(
        jnp.broadcast_to(0.5 * rel, (16, feat)), cf32 * cf32, NT,
        precision=lax.Precision.HIGHEST, preferred_element_type=F32,
    )
    top = half_col.astype(BF).astype(F32)
    mid = (half_col - top).astype(BF).astype(F32)
    bottom = half_col - top - mid
    row_no = lax.broadcasted_iota(jnp.int32, (16, cols), 0)
    colg[mc, pl.ds(cols + npr, 16), :] = jnp.where(
        row_no == 0, top, jnp.where(row_no == 1, mid, jnp.where(row_no == 2, bottom, 0.0))
    ).astype(BF)

    def col_copy(block, to, send):
        return pltpu.make_async_remote_copy(
            src_ref=colg.at[block], dst_ref=colg.at[block],
            send_sem=send, recv_sem=c_recv.at[block],
            device_id=(mr, to), device_id_type=MESH,
        )

    def mate(k):
        return ((chip + k) % n_chip) * 2 + core

    col_sends = [col_copy(mc, mate(n_chip - k), c_send.at[k]) for k in range(1, n_chip)]
    col_sends.append(col_copy(mc, sibling, c_send.at[0]))
    for one in col_sends:
        one.start()

    @pl.loop(1, n_dev)
    def _(off):
        a2a(me, (me + n_dev - off) % n_dev).wait_recv()

    came = got[...].reshape(slots, 128)
    came32 = came.astype(F32)
    spot = came32[:, width : width + 1] * 32.0 + came32[:, width + 1 : width + 2]
    put = (
        spot.astype(jnp.int32) == lax.broadcasted_iota(jnp.int32, (slots, rows), 1) + 1
    ).astype(F32).astype(BF)
    xp = mm(put, came, TN).astype(BF)

    forwards = [col_copy(mate(k), sibling, f_send.at[k]) for k in range(1, n_chip)]

    def forward():
        for k in range(1, n_chip):
            col_copy(mate(k), sibling, f_send.at[k]).wait_recv()
            forwards[k - 1].start()

    rowf[mr] = layers(xp[:, :width], rows, False, forward)

    def row_copy(block, to, send):
        return pltpu.make_async_remote_copy(
            src_ref=rowf.at[block], dst_ref=rowf.at[block],
            send_sem=send, recv_sem=r_recv.at[block],
            device_id=(to, mc), device_id_type=MESH,
        )

    row_sends = [row_copy(mr, (mr + n_row - k) % n_row, r_send.at[k]) for k in range(1, n_row)]
    for one in row_sends:
        one.start()

    for k in range(n_chip):
        other = ((chip + k) % n_chip) * 2 + 1 - core
        col_copy(other, sibling, f_send.at[0]).wait_recv()

    half = rows // 2
    part_sends = []
    for k in range(n_row):
        block = (mr + k) % n_row
        if k:
            row_copy(block, block, r_send.at[0]).wait_recv()
        rf = rowf[block].astype(F32)
        scaled[...] = (rf * rel).astype(BF)
        half_row[...] = jnp.broadcast_to(
            0.5 * jnp.sum(rel * (rf * rf), axis=1, keepdims=True), half_row.shape
        )
        acc[...] = jnp.zeros_like(acc)

        @pl.loop(0, n_col)
        def _(c):
            cross = mm(scaled[...], colg[c, :cols, :], NT)
            sq = colg[c, pl.ds(cols + npr, 16), :].astype(F32)
            sq_col = sq[0:1, :] + sq[1:2, :] + sq[2:3, :]
            kern = jnp.exp(cross - (half_row[...] + sq_col)).astype(BF)
            acc[...] += mm(kern, colg[c, pl.ds(cols, npr), :], NT)

        if k:
            part[k - 1] = jnp.concatenate([acc[:half, :], acc[half:, :]], axis=1).astype(BF)
            one = pltpu.make_async_remote_copy(
                src_ref=part.at[k - 1], dst_ref=parts_in.at[k - 1],
                send_sem=p_send.at[k - 1], recv_sem=p_recv.at[k - 1],
                device_id=(block, mc), device_id_type=MESH,
            )
            one.start()
            part_sends.append(one)
        else:
            out_ref[...] = acc[...]

    for k in range(n_row - 1):
        part_sends[k].wait_recv()
    total = parts_in[0].astype(F32)
    for k in range(1, n_row - 1):
        total += parts_in[k].astype(F32)
    out_ref[:half, :] += total[:, :npr]
    out_ref[half:, :] += total[:, npr:]

    @pl.loop(1, n_dev)
    def _(off):
        a2a((me + off) % n_dev, me).wait_send()

    for one in col_sends + forwards + row_sends + part_sends:
        one.wait_send()


def per_device(n_row, n_col, x, dest, cx, w1, b1, w2, b2, w3, rel, probes):
    n_dev = n_row * n_col
    rows, feat, hid, npr = x.shape[0], w3.shape[1], w1.shape[1], probes.shape[1]
    cols = cx.shape[0] // n_row
    slot = -(-(rows // n_dev) // 16) * 16
    tall = max(rows, cols)
    vmem = pl.BlockSpec(memory_space=pltpu.VMEM)
    hbm = pl.BlockSpec(memory_space=pl.ANY)
    dma = pltpu.SemaphoreType.DMA
    return pl.pallas_call(
        functools.partial(kernel, n_row, n_col, slot),
        out_shape=jax.ShapeDtypeStruct((rows, npr), F32),
        in_specs=[vmem] * 5 + [hbm, vmem, hbm, vmem, vmem],
        out_specs=vmem,
        scratch_shapes=[
            pltpu.VMEM((CHUNKS, hid, hid // CHUNKS), BF),
            pltpu.VMEM((hid, feat), BF),
            pltpu.VMEM((tall, hid), BF),
            pltpu.VMEM((tall, hid), BF),
            pltpu.VMEM((n_dev, slot, 128), BF),
            pltpu.VMEM((n_dev, slot, 128), BF),
            pltpu.VMEM((n_col, cols + npr + 16, feat), BF),
            pltpu.VMEM((n_row, rows, feat), BF),
            pltpu.VMEM((rows, feat), BF),
            pltpu.VMEM((rows, cols), F32),
            pltpu.VMEM((rows, npr), F32),
            pltpu.VMEM((n_row - 1, rows // 2, 2 * npr), BF),
            pltpu.VMEM((n_row - 1, rows // 2, 2 * npr), BF),
            dma((CHUNKS + 1,)),
            dma((n_dev,)),
            dma((n_dev,)),
            dma((n_col // 2,)),
            dma((n_col,)),
            dma((n_col // 2,)),
            dma((n_row,)),
            dma((n_row,)),
            dma((n_row,)),
            dma((n_row,)),
        ],
        compiler_params=pltpu.CompilerParams(
            collective_id=0, has_side_effects=True, vmem_limit_bytes=48 * 2**20
        ),
    )(x, dest.reshape(1, -1), cx, w1, b1.reshape(1, -1), w2, b2.reshape(1, -1), w3,
      rel.reshape(1, -1), probes)


def solution(mesh):
    placed = (
        P(("row", "col"), None),
        P(("row", "col")),
        P("col", None),
        P(),
        P(),
        P(),
        P(),
        P(),
        P(),
        P("col", None),
    )
    return jax.shard_map(
        functools.partial(per_device, mesh.shape["row"], mesh.shape["col"]),
        mesh=mesh, in_specs=placed, out_specs=P(("row", "col"), None), check_vma=False,
    )
```

```python
import functools

import jax
import jax.numpy as jnp
from jax import lax
from jax.experimental import pallas as pl
from jax.experimental.pallas import tpu as pltpu
from jax.sharding import PartitionSpec as P

BF = jnp.bfloat16
F32 = jnp.float32
NN = (((1,), (0,)), ((), ()))
NT = (((1,), (1,)), ((), ()))
TN = (((0,), (0,)), ((), ()))
MESH = pl.DeviceIdType.MESH
CHUNKS = 4


def mm(a, b, dims=NN):
    return lax.dot_general(a, b, dims, preferred_element_type=F32)


def kernel(
    n_row, n_col, slot,
    x_ref, dest_hbm, cx_ref, w1_ref, b1_hbm, w2_hbm, b2_hbm, w3_hbm, rel_hbm, probes_hbm,
    out_ref,
    dest_ref, b1_ref, b2_ref, rel_ref, probes_ref, w2, w3, h1, h2, sent, got, colg, rowf, scaled, half_row, acc, own, part, parts_in,
    in_sem, w_sem, a_send, a_recv, c_send, c_recv, f_send, r_send, r_recv, p_send, p_recv,
):
    n_dev = n_row * n_col
    width, rows = x_ref.shape
    hid = w1_ref.shape[1]
    feat = w3.shape[1]
    npr = probes_ref.shape[0]
    cols = cx_ref.shape[1] // n_row
    step = hid // CHUNKS
    slots = n_dev * slot
    mr, mc = lax.axis_index("row"), lax.axis_index("col")
    me = mr * n_col + mc
    core, chip, n_chip = mc % 2, mc // 2, n_col // 2
    sibling = mc + 1 - 2 * core

    w_copies = [
        pltpu.make_async_copy(w2_hbm.at[:, pl.ds(n * step, step)], w2.at[n], w_sem.at[n])
        for n in range(CHUNKS)
    ]
    w_copies.append(pltpu.make_async_copy(w3_hbm, w3, w_sem.at[CHUNKS]))
    pairs = (
        (dest_hbm, dest_ref), (b1_hbm, b1_ref), (b2_hbm, b2_ref), (rel_hbm, rel_ref),
        (probes_hbm, probes_ref),
    )
    in_copies = [
        pltpu.make_async_copy(src, dst, in_sem.at[n]) for n, (src, dst) in enumerate(pairs)
    ]
    for one in in_copies + w_copies:
        one.start()

    barrier = pltpu.get_barrier_semaphore()

    @pl.loop(1, n_dev)
    def _(off):
        to = (me + off) % n_dev
        pl.semaphore_signal(
            barrier, inc=1, device_id=(to // n_col, to % n_col), device_id_type=MESH
        )

    in_copies[0].wait()
    bits = rows.bit_length() - 1
    dest = dest_ref[...]
    target = lax.shift_right_logical(dest, jnp.full_like(dest, bits))
    place = lax.bitwise_and(dest, jnp.full_like(dest, rows - 1)) + 1
    one_hot = (lax.broadcasted_iota(jnp.int32, (n_dev, rows), 0) == target).astype(F32)
    before = (
        lax.broadcasted_iota(jnp.int32, (rows, rows), 0)
        < lax.broadcasted_iota(jnp.int32, (rows, rows), 1)
    ).astype(F32).astype(BF)
    count = mm(one_hot.astype(BF), before)
    within = jnp.sum(one_hot * count, axis=0, keepdims=True)
    key = target * slot + within.astype(jnp.int32)
    pick = (lax.broadcasted_iota(jnp.int32, (slots, rows), 0) == key).astype(F32).astype(BF)
    high = lax.shift_right_logical(place, jnp.full_like(place, 5)).astype(F32)
    low = lax.bitwise_and(place, jnp.full_like(place, 31)).astype(F32)
    line = lax.broadcasted_iota(jnp.int32, (128, rows), 0)
    marks = jnp.where(line == width, high, jnp.where(line == width + 1, low, 0.0)).astype(BF)
    sent[...] = mm(pick, marks, NT).astype(BF).reshape(n_dev, slot, 128)
    sent[:, :, :width] = mm(pick, x_ref[...], NT).astype(BF).reshape(n_dev, slot, width)
    got[me] = sent[me]

    pl.semaphore_wait(barrier, n_dev - 1)

    def a2a(to, sem_at):
        return pltpu.make_async_remote_copy(
            src_ref=sent.at[to], dst_ref=got.at[sem_at],
            send_sem=a_send.at[to], recv_sem=a_recv.at[sem_at],
            device_id=(to // n_col, to % n_col), device_id_type=MESH,
        )

    @pl.loop(1, n_dev)
    def _(off):
        a2a((me + off) % n_dev, me).start()

    def layers(x, m, first, dims):
        for n in range(CHUNKS):
            at = pl.ds(n * step, step)
            h1[:m, at] = jnp.maximum(mm(x, w1_ref[:, at], dims) + b1_ref[:, at], 0.0).astype(BF)
        if first:
            for one in w_copies[:CHUNKS]:
                one.wait()

        @pl.loop(0, CHUNKS)
        def _(n):
            at = pl.ds(pl.multiple_of(n * step, step), step)
            h2[:m, at] = jnp.maximum(mm(h1[:m, :], w2[n]) + b2_ref[:, at], 0.0).astype(BF)

        if first:
            w_copies[CHUNKS].wait()
        return mm(h2[:m, :], w3[...]).astype(BF)

    mine = pl.ds(pl.multiple_of(mr * cols, cols), cols)
    for one in in_copies[1:]:
        one.wait()
    rel = rel_ref[...]
    cf = layers(cx_ref[:, mine], cols, True, TN)
    colg[mc, :cols, :] = cf
    colg[mc, pl.ds(cols, npr), :] = probes_ref[:, mine].astype(BF)
    cf32 = cf.astype(F32)
    half_col = lax.dot_general(
        jnp.broadcast_to(0.5 * rel, (16, feat)), cf32 * cf32, NT,
        precision=lax.Precision.HIGHEST, preferred_element_type=F32,
    )
    top = half_col.astype(BF).astype(F32)
    mid = (half_col - top).astype(BF).astype(F32)
    bottom = half_col - top - mid
    row_no = lax.broadcasted_iota(jnp.int32, (16, cols), 0)
    colg[mc, pl.ds(cols + npr, 16), :] = jnp.where(
        row_no == 0, top, jnp.where(row_no == 1, mid, jnp.where(row_no == 2, bottom, 0.0))
    ).astype(BF)

    def col_copy(block, to, send):
        return pltpu.make_async_remote_copy(
            src_ref=colg.at[block], dst_ref=colg.at[block],
            send_sem=send, recv_sem=c_recv.at[block],
            device_id=(mr, to), device_id_type=MESH,
        )

    def mate(k):
        return ((chip + k) % n_chip) * 2 + core

    col_sends = [col_copy(mc, mate(n_chip - k), c_send.at[k]) for k in range(1, n_chip)]
    col_sends.append(col_copy(mc, sibling, c_send.at[0]))
    for one in col_sends:
        one.start()

    @pl.loop(1, n_dev)
    def _(off):
        a2a(me, (me + n_dev - off) % n_dev).wait_recv()

    came = got[...].reshape(slots, 128)
    came32 = came.astype(F32)
    spot = came32[:, width : width + 1] * 32.0 + came32[:, width + 1 : width + 2]
    put = (
        spot.astype(jnp.int32) == lax.broadcasted_iota(jnp.int32, (slots, rows), 1) + 1
    ).astype(F32).astype(BF)
    xp = mm(put, came, TN).astype(BF)

    forwards = [col_copy(mate(k), sibling, f_send.at[k]) for k in range(1, n_chip)]

    rowf[mr] = layers(xp[:, :width], rows, False, NN)

    def row_copy(block, to, send):
        return pltpu.make_async_remote_copy(
            src_ref=rowf.at[block], dst_ref=rowf.at[block],
            send_sem=send, recv_sem=r_recv.at[block],
            device_id=(to, mc), device_id_type=MESH,
        )

    row_sends = [row_copy(mr, (mr + n_row - k) % n_row, r_send.at[k]) for k in range(1, n_row)]
    for one in row_sends:
        one.start()

    for k in range(1, n_chip):
        col_copy(mate(k), sibling, f_send.at[k]).wait_recv()
        forwards[k - 1].start()

    for k in range(n_chip):
        other = ((chip + k) % n_chip) * 2 + 1 - core
        col_copy(other, sibling, f_send.at[0]).wait_recv()

    half = rows // 2
    part_sends = []
    for k in range(n_row):
        block = (mr + k) % n_row
        if k:
            row_copy(block, block, r_send.at[0]).wait_recv()
        rf = rowf[block].astype(F32)
        scaled[...] = (rf * rel).astype(BF)
        half_row[...] = jnp.broadcast_to(
            0.5 * jnp.sum(rel * (rf * rf), axis=1, keepdims=True), half_row.shape
        )
        acc[...] = jnp.zeros_like(acc)

        @pl.loop(0, n_col, unroll=2)
        def _(c):
            cross = mm(scaled[...], colg[c, :cols, :], NT)
            sq = colg[c, pl.ds(cols + npr, 16), :].astype(F32)
            sq_col = sq[0:1, :] + sq[1:2, :] + sq[2:3, :]
            kern = jnp.exp(cross - (half_row[...] + sq_col)).astype(BF)
            acc[...] += mm(kern, colg[c, pl.ds(cols, npr), :], NT)

        if k:
            part[k - 1] = jnp.concatenate([acc[:half, :], acc[half:, :]], axis=1).astype(BF)
            one = pltpu.make_async_remote_copy(
                src_ref=part.at[k - 1], dst_ref=parts_in.at[k - 1],
                send_sem=p_send.at[k - 1], recv_sem=p_recv.at[k - 1],
                device_id=(block, mc), device_id_type=MESH,
            )
            one.start()
            part_sends.append(one)
        else:
            own[...] = acc[...]

    for k in range(n_row - 1):
        part_sends[k].wait_recv()
    total = parts_in[0].astype(F32)
    for k in range(1, n_row - 1):
        total += parts_in[k].astype(F32)
    own[:half, :] += total[:, :npr]
    own[half:, :] += total[:, npr:]
    out_ref[...] = own[...].T

    @pl.loop(1, n_dev)
    def _(off):
        a2a((me + off) % n_dev, me).wait_send()

    for one in col_sends + forwards + row_sends + part_sends:
        one.wait_send()


def per_device(n_row, n_col, x, dest, cx, w1, b1, w2, b2, w3, rel, probes):
    n_dev = n_row * n_col
    rows, feat, hid, npr = x.shape[0], w3.shape[1], w1.shape[1], probes.shape[1]
    cols = cx.shape[0] // n_row
    slot = -(-(rows // n_dev) // 16) * 16
    tall = max(rows, cols)
    vmem = pl.BlockSpec(memory_space=pltpu.VMEM)
    hbm = pl.BlockSpec(memory_space=pltpu.HBM)
    dma = pltpu.SemaphoreType.DMA
    return pl.pallas_call(
        functools.partial(kernel, n_row, n_col, slot),
        out_shape=jax.ShapeDtypeStruct((npr, rows), F32),
        in_specs=[vmem, hbm, vmem, vmem] + [hbm] * 6,
        out_specs=vmem,
        scratch_shapes=[
            pltpu.VMEM((1, rows), jnp.int32),
            pltpu.VMEM((1, hid), F32),
            pltpu.VMEM((1, hid), F32),
            pltpu.VMEM((1, feat), F32),
            pltpu.VMEM((npr, cols * n_row), F32),
            pltpu.VMEM((CHUNKS, hid, hid // CHUNKS), BF),
            pltpu.VMEM((hid, feat), BF),
            pltpu.VMEM((tall, hid), BF),
            pltpu.VMEM((tall, hid), BF),
            pltpu.VMEM((n_dev, slot, 128), BF),
            pltpu.VMEM((n_dev, slot, 128), BF),
            pltpu.VMEM((n_col, cols + npr + 16, feat), BF),
            pltpu.VMEM((n_row, rows, feat), BF),
            pltpu.VMEM((rows, feat), BF),
            pltpu.VMEM((rows, cols), F32),
            pltpu.VMEM((rows, npr), F32),
            pltpu.VMEM((rows, npr), F32),
            pltpu.VMEM((n_row - 1, rows // 2, 2 * npr), BF),
            pltpu.VMEM((n_row - 1, rows // 2, 2 * npr), BF),
            dma((5,)),
            dma((CHUNKS + 1,)),
            dma((n_dev,)),
            dma((n_dev,)),
            dma((n_col // 2,)),
            dma((n_col,)),
            dma((n_col // 2,)),
            dma((n_row,)),
            dma((n_row,)),
            dma((n_row,)),
            dma((n_row,)),
        ],
        compiler_params=pltpu.CompilerParams(
            collective_id=0, has_side_effects=True, vmem_limit_bytes=60 * 2**20
        ),
    )(x.T, dest.reshape(1, -1), cx.T, w1, b1.reshape(1, -1), w2, b2.reshape(1, -1), w3,
      rel.reshape(1, -1), probes.T).T


def solution(mesh):
    placed = (
        P(("row", "col"), None),
        P(("row", "col")),
        P("col", None),
        P(),
        P(),
        P(),
        P(),
        P(),
        P(),
        P("col", None),
    )
    return jax.shard_map(
        functools.partial(per_device, mesh.shape["row"], mesh.shape["col"]),
        mesh=mesh, in_specs=placed, out_specs=P(("row", "col"), None), check_vma=False,
    )
```
